32 devices in a mesh: chan: 8 (over y, x, core), tile: 4 (over z).
Axes of the slice: x: 2, y: 2, z: 4, core: 2. Of those that a mesh axis runs over, the one named last changes fastest.
Arguments:
- visibility: float32 [2, 8192], P(None, ('chan', 'tile')), may hold values from -6 to 6
- kernel_table: bfloat16 [2048, 128], replicated, may hold values from -0.8984375 to 0.8984375
- cell_index: int32 [8192], P(('chan', 'tile')), may hold values from 0 to 65535
- tile_index: int32 [8192, 1], P(('chan', 'tile')), may hold values from 0 to 3; in each aligned block of 256 rows (0 to 255, 256 to 511, ...) at most 128 rows name the same one
- plane_index: int32 [8192], P(('chan', 'tile')), may hold values from 0 to 31
- offset_index: int32 [8192], P(('chan', 'tile')), may hold values from 0 to 63
Outputs:
- gridded: float32 [2, 64, 4096], P(None, 'tile', 'chan')
The draws below stay inside these ranges and needn't reach their ends.
Inputs may be any that keep to these rules, and one draw needn't show every extreme that they name: `tile_index`: among the rows of one device at most 128 name the same tile, and in some device some tile is named by exactly 128 rows.
All inputs are finite; a program needn't handle non-finite values.
Results may differ from the reference program's by a relative error of at most 0.0029.
Values may be sent and summed in bfloat16 or wider, within the bound.
No kernel may reach another device: no remote copies, remote signals or barrier semaphores. Data moves between devices by JAX's collectives and lax.ppermute only.
A program may use at most 64 MiB of HBM per device.

```python
import math
import jax
import jax.numpy as jnp
import numpy as np
from jax import lax

GRID_U = 4096
SUPPORT = 8
OVERSAMPLE = 8
PLANES = 32
TILE_V = 16
CAPACITY = 128
ROWS_DEV = 256
ROWS = 8192
BAND_V = 64
KERNELS = 2048
N_TILE = 4


def with_ends(values, key, least, top_value):
    shape = values.shape
    place = [jax.random.randint(jax.random.fold_in(key, axis), (), 0, shape[axis]) for axis in range(len(shape))]
    values = values.at[tuple(place)].set(least)
    longest = shape.index(max(shape))
    place[longest] = (place[longest] + 1) % shape[longest]
    return values.at[tuple(place)].set(top_value)


def steps_of(rng, extent, split, least, largest):
    factor_of, own = 1.0, jax.random.fold_in(rng, 6)
    for axis_at, blocks in split:
        draws = jnp.exp(jax.random.uniform(jax.random.fold_in(own, axis_at), (blocks,), jnp.float32, least / len(split), largest / len(split)))
        factor_of = factor_of * jnp.repeat(draws, extent[axis_at] // blocks).reshape([-1 if axis == axis_at else 1 for axis in range(len(extent))])
    return factor_of


def shared_out(own_key, own, number, rows, number_of, top, bound, skew):
    ranking = jax.random.permutation(own_key, number_of)
    packed, usual = load_shares(number_of, rows * top, bound, skew, True), load_shares(number_of, rows * top, bound, skew, False)
    places = jnp.arange(number_of)

    def named(sizes, rotation):
        used = int((sizes > 0).sum())
        fixed = max(1, used // 4)
        passed = fixed + (places - fixed + rotation * (used - fixed)) % max(1, number_of - fixed)
        return jnp.zeros((number_of,), jnp.int32).at[ranking[jnp.where(places < fixed, places, passed)]].set(jnp.asarray(sizes, jnp.int32))

    sizes = jnp.where(number % 4 == 0, named(packed, number // 4), named(usual, number - number // 4 - 1))
    mixed = jax.random.permutation(jax.random.fold_in(own, 3), number_of)
    giver, receiver = mixed[0:number_of // 2 * 2:2], mixed[1:number_of // 2 * 2:2]
    margin = jnp.minimum(sizes[giver] - 1, bound - sizes[receiver]) // 2
    margin = jnp.where((giver == ranking[0]) | (receiver == ranking[0]) | (sizes[receiver] == 0), 0, jnp.maximum(margin, 0))
    passed = jax.random.randint(jax.random.fold_in(own, 4), (number_of // 2,), 0, 1 << 20) % (margin + 1)
    sizes = sizes.at[giver].add(-passed).at[receiver].add(passed)
    items = jnp.searchsorted(jnp.cumsum(sizes), jnp.arange(rows * top), side="right").astype(jnp.int32)
    table = items.reshape(top, rows).T
    table = table[jax.random.permutation(jax.random.fold_in(own, 1), rows)]
    rotation = jax.random.randint(jax.random.fold_in(own, 2), (rows, 1), 0, top)
    return jnp.take_along_axis(table, (jnp.arange(top)[None, :] + rotation) % top, axis=1)


def load_shares(amount, total, limit, skew, full):
    portions = [(1 << 20) // math.isqrt(grade ** skew) + 1 for grade in range(1, amount + 1)]
    largest = limit if full else min(limit, max(-(-total // amount), total * portions[0] // sum(portions)))
    least = 1 if total - largest >= amount - 1 else 0
    holding, spare = [largest] + [least] * (amount - 1), total - largest - least * (amount - 1)
    while spare > 0:
        candidates = [i for i in range(1, amount) if holding[i] < largest] or [i for i in range(1, amount) if holding[i] < limit]
        whole, remaining = sum([portions[i] for i in candidates]), spare
        for i in candidates:
            extra = min(limit - holding[i], max(1, remaining * portions[i] // whole), spare)
            holding[i] = holding[i] + extra
            spare = spare - extra
    return np.array(holding)


def centred(key, shape, scale, reach, shards=(), kind=jnp.bfloat16):
    gain = steps_of(key, shape, shards, -0.22, 0.18) if shards else 1.0
    result = jax.random.normal(key, shape, jnp.float32) * scale * gain
    return jnp.minimum(jnp.maximum(result, -reach), reach).astype(kind)


def setup_inputs(seed: int = 0) -> dict:
    seeds = jax.random.split(jax.random.key(seed), 7)
    visibility = centred(seeds[0], (2, ROWS), 1.0, 6.0, ((1, 32),), jnp.float32)
    kernel_table = centred(seeds[1], (KERNELS, 2 * SUPPORT * SUPPORT), 0.15, 0.8984375)
    cell_index = with_ends(jax.random.randint(seeds[2], (ROWS,), 0, TILE_V * GRID_U), jax.random.fold_in(seeds[2], 1), 0, (TILE_V * GRID_U) - 1).astype(jnp.int32)
    tile_index_keys = jax.random.split(jax.random.fold_in(seeds[3], 1), ROWS // ROWS_DEV)
    tile_index_turns = jax.random.permutation(jax.random.fold_in(seeds[3], 3), ROWS // ROWS_DEV)
    tile_index = jax.vmap(lambda own, number: shared_out(jax.random.fold_in(seeds[3], 2), own, number, ROWS_DEV, N_TILE, 1, CAPACITY, 2))(tile_index_keys, tile_index_turns).reshape((ROWS, 1))
    plane_index = with_ends(jax.random.randint(seeds[4], (ROWS,), 0, PLANES), jax.random.fold_in(seeds[4], 1), 0, PLANES - 1).astype(jnp.int32)
    offset_index = with_ends(jax.random.randint(seeds[5], (ROWS,), 0, OVERSAMPLE * OVERSAMPLE), jax.random.fold_in(seeds[5], 1), 0, (OVERSAMPLE * OVERSAMPLE) - 1).astype(jnp.int32)
    return dict(visibility=visibility, kernel_table=kernel_table, cell_index=cell_index, tile_index=tile_index, plane_index=plane_index, offset_index=offset_index)


def reference(visibility, kernel_table, cell_index, tile_index, plane_index, offset_index):
    kind = plane_index * (OVERSAMPLE * OVERSAMPLE) + offset_index
    area = SUPPORT * SUPPORT
    blocks = ROWS // ROWS_DEV
    vis_blocks = visibility.reshape(2, blocks, ROWS_DEV).transpose(1, 0, 2)
    kind_blocks = kind.reshape(blocks, ROWS_DEV)
    cell_blocks = cell_index.reshape(blocks, ROWS_DEV)
    tile_blocks = tile_index[:, 0].reshape(blocks, ROWS_DEV)
    taps = jnp.arange(SUPPORT, dtype=jnp.int32)

    def step(grid, pieces):
        vis_part, kind_part, cell_part, tile_part = pieces
        kern = kernel_table[kind_part].astype(jnp.float32)
        real_kern = kern[:, :area]
        imag_kern = kern[:, area:]
        vis_real = vis_part[0][:, None]
        vis_imag = vis_part[1][:, None]
        real_part = (vis_real * real_kern - vis_imag * imag_kern).astype(jnp.bfloat16)
        imag_part = (vis_real * imag_kern + vis_imag * real_kern).astype(jnp.bfloat16)
        real_part, imag_part = lax.optimization_barrier((real_part, imag_part))
        real_part = real_part.astype(jnp.float32).reshape(-1, SUPPORT, SUPPORT)
        imag_part = imag_part.astype(jnp.float32).reshape(-1, SUPPORT, SUPPORT)
        row_pos = tile_part * TILE_V + cell_part // GRID_U
        col_pos = cell_part % GRID_U
        ys = jnp.broadcast_to(row_pos[:, None, None] + taps[None, None, :], real_part.shape).astype(jnp.int32)
        xs = jnp.broadcast_to(col_pos[:, None, None] + taps[None, :, None], real_part.shape).astype(jnp.int32)
        grid = grid.at[0, ys, xs].add(real_part, mode="drop")
        grid = grid.at[1, ys, xs].add(imag_part, mode="drop")
        return grid, None

    start = jnp.zeros((2, BAND_V, GRID_U), jnp.float32)
    grid, _ = lax.scan(step, start, (vis_blocks, kind_blocks, cell_blocks, tile_blocks))
    return grid
```

```python
import functools

import jax
import jax.numpy as jnp
from jax import lax
from jax.experimental import pallas as pl
from jax.experimental.pallas import tpu as pltpu
from jax.sharding import PartitionSpec as P

GRID_U = 4096
SUPPORT = 8
OVERSAMPLE = 8
TILE_V = 16
AREA = SUPPORT * SUPPORT
LANES = 128
BLOCK = 2 * LANES
CHUNK = 768
PIECE = 256


def pack_kernel(vis_ref, cell_ref, tile_ref, plane_ref, offset_ref, out_ref):
    rows = vis_ref.shape[1]
    address = (tile_ref[...] * (TILE_V * GRID_U) + cell_ref[...]).astype(jnp.float32)
    kind = (plane_ref[...] * (OVERSAMPLE * OVERSAMPLE) + offset_ref[...]).astype(jnp.float32)
    parts = []
    for first in range(0, rows, BLOCK):
        for q in range(2):
            for half in range(2):
                start = first + half * LANES
                parts.append(vis_ref[q : q + 1, start : start + LANES])
        at = first // LANES
        parts.append(address[at : at + 2])
        parts.append(kind[at : at + 2])
    packed = jnp.concatenate(parts, axis=0)

    @pl.loop(0, out_ref.shape[0])
    def _(d):
        out_ref[d] = packed


def pack(devices, visibility, cell, tile, plane, offset):
    rows = visibility.shape[1]
    flat = [a.reshape(rows // LANES, LANES) for a in (cell, tile, plane, offset)]
    return pl.pallas_call(
        pack_kernel,
        out_shape=jax.ShapeDtypeStruct((devices, rows // BLOCK * 8, LANES), jnp.float32),
        in_specs=[pl.BlockSpec(memory_space=pltpu.VMEM)] * 5,
        out_specs=pl.BlockSpec(memory_space=pltpu.VMEM),
        compiler_params=pltpu.CompilerParams(vmem_limit_bytes=32 * 1024 * 1024),
    )(visibility, *flat)


def along_lanes(values, index):
    return jnp.take_along_axis(values, index, axis=1, mode="promise_in_bounds")


def along_sublanes(values, index):
    return jnp.take_along_axis(values, index, axis=0, mode="promise_in_bounds")


def iota(shape, axis):
    return lax.broadcasted_iota(jnp.int32, shape, axis)


def dot(a, b, dims):
    return lax.dot_general(a, b, (dims, ((), ())), preferred_element_type=jnp.float32)


def grid_kernel(span, rows_ref, table_ref, out_ref, total_ref):
    width = out_ref.shape[2]
    blocks = rows_ref.shape[0] // 8
    groups = 2 * span
    first_u = lax.axis_index("chan") * width
    first_v = lax.axis_index("tile") * TILE_V
    total_ref[...] = jnp.zeros_like(total_ref)
    upper = (iota((LANES, LANES), 0) <= iota((LANES, LANES), 1)).astype(jnp.float32).astype(jnp.bfloat16)
    ones = jnp.ones((LANES, LANES), jnp.bfloat16)
    before = (iota((groups, groups), 1) < iota((groups, groups), 0)).astype(jnp.float32).astype(jnp.bfloat16)

    def section(first_block):
        def column(q):
            return jnp.concatenate(
                [rows_ref[pl.ds(first_block * 8 + q * 2 + half, span, stride=8), :] for half in range(2)],
                axis=0,
            )

        real, imag, address, kind = [column(q) for q in range(4)]
        whole = address.astype(jnp.int32)
        v_rel = (whole >> 12) - first_v
        u_rel = (whole & (GRID_U - 1)) - first_u
        touches = (v_rel > -SUPPORT) & (v_rel < TILE_V) & (u_rel > -SUPPORT) & (u_rel < width)
        marks = jnp.where(touches, 1.0, 0.0).astype(jnp.bfloat16)
        upto = dot(marks, upper, ((1,), (0,))).astype(jnp.int32)
        count = dot(marks, ones, ((1,), (0,)))
        base = dot(before, count.astype(jnp.bfloat16), ((1,), (0,))).astype(jnp.int32)
        count = count.astype(jnp.int32)
        picked = jnp.max(base + count)
        lane = iota((groups, LANES), 1)
        source = jnp.zeros((groups, LANES), jnp.int32)
        step = LANES // 2
        while step:
            probe = along_lanes(upto, source + (step - 1))
            source = jnp.where(probe <= lane, source + step, source)
            step //= 2

        def chunk(number, carry):
            lists = [[], [], [], []]
            for piece in range(CHUNK // LANES):
                place = lane + (number * CHUNK + piece * LANES) - base
                here = (place >= 0) & (place < count)
                at = along_lanes(source, place & (LANES - 1))
                for q, values in enumerate((real, imag, address, kind)):
                    got = jnp.where(here, along_lanes(values, at), 0.0)
                    lists[q].append(jnp.sum(got, axis=0, keepdims=True))
            for piece in range(CHUNK // PIECE):
                each = PIECE // LANES
                vr, vi, address_n, kind_n = [
                    jnp.concatenate(l[piece * each : (piece + 1) * each], axis=1) for l in lists
                ]
                whole_n = address_n.astype(jnp.int32)
                v_n = (whole_n >> 12) - first_v
                u_n = (whole_n & (GRID_U - 1)) - first_u
                kind_i = kind_n.astype(jnp.int32)
                low = kind_i & 255
                high = kind_i >> 8
                onehot = jnp.where(iota((256, PIECE), 0) == low, 1.0, 0.0).astype(jnp.bfloat16)
                kern = jnp.zeros((2 * AREA, PIECE), jnp.float32)
                for t in range(table_ref.shape[0] // (2 * AREA)):
                    part = dot(table_ref[t * 2 * AREA : (t + 1) * 2 * AREA, :], onehot, ((1,), (0,)))
                    kern = kern + jnp.where(high == t, part, 0.0)
                real_kern = kern[:AREA]
                imag_kern = kern[AREA:]
                weighted = (vr * real_kern - vi * imag_kern, vr * imag_kern + vi * real_kern)
                sub = iota((SUPPORT, PIECE), 0)
                turn = (sub - v_n) & (SUPPORT - 1)
                inside = [(sub + 8 * y >= v_n) & (sub + 8 * y < v_n + SUPPORT) for y in range(2)]
                spread = []
                for i in range(SUPPORT):
                    in_u = (u_n + i >= 0) & (u_n + i < width)
                    for c in range(2):
                        turned = along_sublanes(weighted[c][i * 8 : (i + 1) * 8], turn)
                        for y in range(2):
                            spread.append(jnp.where(inside[y] & in_u, turned, 0.0))
                spread = jnp.concatenate(spread, axis=0).astype(jnp.bfloat16)
                column_n = jnp.where(u_n < 0, u_n + width, u_n)
                place_u = jnp.where(iota((width, PIECE), 0) == column_n, 1.0, 0.0).astype(jnp.bfloat16)
                total_ref[...] += dot(spread, place_u, ((1,), (1,)))
            return carry

        lax.fori_loop(0, (picked + CHUNK - 1) // CHUNK, chunk, 0)

    if blocks == span:
        section(0)
    else:
        pl.loop(0, blocks // span)(lambda s: section(s * span))
    both = 2 * TILE_V
    result = total_ref[0:both, :]
    for i in range(1, SUPPORT):
        result = result + pltpu.roll(total_ref[i * both : (i + 1) * both, :], i, axis=1)
    out_ref[0] = result[:TILE_V]
    out_ref[1] = result[TILE_V:]


def body(visibility, kernel_table, cell_index, tile_index, plane_index, offset_index):
    chans, tiles = lax.axis_size("chan"), lax.axis_size("tile")
    devices = chans * tiles
    packed = pack(devices, visibility, cell_index, tile_index[:, 0], plane_index, offset_index)
    arrived = lax.all_to_all(packed, ("chan", "tile"), split_axis=0, concat_axis=0)
    kernels = kernel_table.shape[0]
    table = kernel_table.reshape(kernels // 256, 256, 2 * AREA).transpose(0, 2, 1).reshape(-1, 256)
    rows = arrived.reshape(-1, LANES)
    blocks = rows.shape[0] // 8
    span = 32 if blocks % 32 == 0 else blocks
    width = GRID_U // chans
    return pl.pallas_call(
        functools.partial(grid_kernel, span),
        out_shape=jax.ShapeDtypeStruct((2, TILE_V, width), jnp.float32),
        in_specs=[pl.BlockSpec(memory_space=pltpu.VMEM)] * 2,
        out_specs=pl.BlockSpec(memory_space=pltpu.VMEM),
        scratch_shapes=[pltpu.VMEM((2 * TILE_V * SUPPORT, width), jnp.float32)],
        compiler_params=pltpu.CompilerParams(vmem_limit_bytes=32 * 1024 * 1024),
    )(rows, table)


def solution(mesh):
    placed = (
        P(None, ("chan", "tile")),
        P(),
        P(("chan", "tile")),
        P(("chan", "tile"), None),
        P(("chan", "tile")),
        P(("chan", "tile")),
    )
    return jax.shard_map(
        body, mesh=mesh, in_specs=placed, out_specs=P(None, "tile", "chan"), check_vma=False
    )
```

```python
import functools

import jax
import jax.numpy as jnp
from jax import lax
from jax.experimental import pallas as pl
from jax.experimental.pallas import tpu as pltpu
from jax.sharding import PartitionSpec as P

GRID_U = 4096
SUPPORT = 8
OVERSAMPLE = 8
TILE_V = 16
AREA = SUPPORT * SUPPORT
LANES = 128
BLOCK = 2 * LANES
PLAIN = 4
PIECE = 256


def pack_kernel(vis_ref, cell_ref, tile_ref, plane_ref, offset_ref, out_ref):
    rows = vis_ref.shape[1]
    address = (tile_ref[...] * (TILE_V * GRID_U) + cell_ref[...]).astype(jnp.float32)
    kind = (plane_ref[...] * (OVERSAMPLE * OVERSAMPLE) + offset_ref[...]).astype(jnp.float32)
    parts = []
    for first in range(0, rows, BLOCK):
        for q in range(2):
            for half in range(2):
                start = first + half * LANES
                parts.append(vis_ref[q : q + 1, start : start + LANES])
        at = first // LANES
        parts.append(address[at : at + 2])
        parts.append(kind[at : at + 2])
    packed = jnp.concatenate(parts, axis=0)

    for d in range(out_ref.shape[0]):
        out_ref[d] = packed


def pack(devices, visibility, cell, tile, plane, offset):
    rows = visibility.shape[1]
    flat = [a.reshape(rows // LANES, LANES) for a in (cell, tile, plane, offset)]
    return pl.pallas_call(
        pack_kernel,
        out_shape=jax.ShapeDtypeStruct((devices, rows // BLOCK * 8, LANES), jnp.float32),
        in_specs=[pl.BlockSpec(memory_space=pltpu.VMEM)] * 5,
        out_specs=pl.BlockSpec(memory_space=pltpu.VMEM),
        compiler_params=pltpu.CompilerParams(vmem_limit_bytes=4 * 1024 * 1024),
    )(visibility, *flat)


def along_lanes(values, index):
    return jnp.take_along_axis(values, index, axis=1, mode="promise_in_bounds")


def along_sublanes(values, index):
    return jnp.take_along_axis(values, index, axis=0, mode="promise_in_bounds")


def iota(shape, axis):
    return lax.broadcasted_iota(jnp.int32, shape, axis)


def dot(a, b, dims):
    return lax.dot_general(a, b, (dims, ((), ())), preferred_element_type=jnp.float32)


def ranks_down(marks):
    sub = iota((8, LANES), 0)
    above = jnp.zeros((8, LANES), jnp.int32)
    ranks = []
    for tile in marks:
        run = tile
        for by in (1, 2, 4):
            run = run + jnp.where(sub >= by, pltpu.roll(run, by, axis=0), 0)
        ranks.append(above + run - tile)
        above = above + jnp.broadcast_to(run[7:8], run.shape)
    return ranks, above


def grid_kernel(span, rows_ref, table_ref, out_ref, total_ref):
    width = out_ref.shape[2]
    blocks = rows_ref.shape[0] // 8
    first_u = lax.axis_index("chan") * width
    first_v = lax.axis_index("tile") * TILE_V
    sub = iota((8, LANES), 0)

    def section(first_block, fresh):
        def column(q, first):
            return rows_ref[pl.ds(first_block * 8 + first * 8 + q, 8, stride=8), :]

        real, imag, code, marks = [], [], [], []
        for half in range(2):
            for first in range(0, span, 8):
                real.append(column(half, first))
                imag.append(column(2 + half, first))
                address = column(4 + half, first).astype(jnp.int32)
                kind = column(6 + half, first).astype(jnp.int32)
                v_rel = (address >> 12) - first_v
                u_rel = (address & (GRID_U - 1)) - first_u
                touches = (v_rel > -SUPPORT) & (v_rel < TILE_V) & (u_rel > -SUPPORT) & (u_rel < width)
                marks.append(jnp.where(touches, 1, 0))
                code.append(kind + ((u_rel + SUPPORT) << 11) + ((v_rel + SUPPORT) << 24))
        ranks, total = ranks_down(marks)
        ranks = [jnp.where(m > 0, r, -1) for m, r in zip(marks, ranks)]
        lines = [[jnp.broadcast_to(r[j : j + 1], r.shape) for j in range(8)] for r in ranks]

        def pick(wanted):
            got = [jnp.zeros((8, LANES), x[0].dtype) for x in (real, imag, code)]
            for k, line in enumerate(lines):
                source = jnp.full((8, LANES), -1, jnp.int32)
                for j in range(8):
                    source = jnp.where(line[j] == wanted, j, source)
                for q, x in enumerate((real, imag, code)):
                    got[q] = jnp.where(source >= 0, along_sublanes(x[k], source & 7), got[q])
            return got

        def split(tiles, count):
            return [[tiles[q][r : r + 1] for r in range(count)] for q in range(3)]

        def add_up(lists, fresh):
            spreads, places = [], []
            for first in range(0, len(lists[0]), PIECE // LANES):
                vr, vi, code_n = [jnp.concatenate(l[first : first + PIECE // LANES], axis=1) for l in lists]
                kind_n = code_n & 2047
                u_n = ((code_n >> 11) & 8191) - SUPPORT
                v_n = (code_n >> 24) - SUPPORT
                low = kind_n & 255
                high = kind_n >> 8
                onehot = jnp.where(iota((256, PIECE), 0) == low, 1.0, 0.0).astype(jnp.bfloat16)
                kern = jnp.zeros((2 * AREA, PIECE), jnp.float32)
                for t in range(table_ref.shape[0] // (2 * AREA)):
                    part = dot(table_ref[t * 2 * AREA : (t + 1) * 2 * AREA, :], onehot, ((1,), (0,)))
                    kern = jnp.where(high == t, part, kern)
                real_kern = kern[:AREA]
                imag_kern = kern[AREA:]
                weighted = (vr * real_kern - vi * imag_kern, vr * imag_kern + vi * real_kern)
                sub_n = iota((SUPPORT, PIECE), 0)
                turn = (sub_n - v_n) & (SUPPORT - 1)
                inside = [(sub_n + 8 * y >= v_n) & (sub_n + 8 * y < v_n + SUPPORT) for y in range(2)]
                spread = []
                for i in range(SUPPORT):
                    in_u = (u_n + i >= 0) & (u_n + i < width)
                    for c in range(2):
                        turned = along_sublanes(weighted[c][i * 8 : (i + 1) * 8], turn)
                        for y in range(2):
                            spread.append(jnp.where(inside[y] & in_u, turned, 0.0))
                spreads.append(jnp.concatenate(spread, axis=0).astype(jnp.bfloat16))
                column_n = jnp.where(u_n < 0, u_n + width, u_n)
                places.append(jnp.where(iota((width, PIECE), 0) == column_n, 1.0, 0.0).astype(jnp.bfloat16))
            sums = dot(jnp.concatenate(spreads, axis=1), jnp.concatenate(places, axis=1), ((1,), (1,)))
            if fresh:
                total_ref[...] = sums
            else:
                total_ref[...] += sums

        beyond = jnp.maximum(total - PLAIN, 0)
        lane = iota((LANES, LANES), 0)
        other = iota((LANES, LANES), 1)
        left = jnp.where(((lane & 15) == (other & 15)) & (lane < other), 1.0, 0.0).astype(jnp.bfloat16)
        skip = dot(beyond.astype(jnp.float32).astype(jnp.bfloat16), left, ((1,), (0,))).astype(jnp.int32)
        lists = split(pick(sub), PLAIN)
        group = iota((8, LANES), 1) >> 4
        for first in (0, 8):
            wanted = sub + first - skip
            shared = pick(jnp.where(wanted >= 0, wanted + PLAIN, -2))
            for q, x in enumerate(shared):
                for by in (16, 32, 64):
                    x = x + pltpu.roll(x, by, axis=1)
                x = jnp.where(group == sub, x, jnp.zeros_like(x))
                for by in (1, 2, 4):
                    x = x + pltpu.roll(x, by, axis=0)
                lists[q].append(x[0:1])
        add_up(lists, fresh)
        done = PLAIN + jnp.maximum(16 - skip, 0)
        most = jnp.max(total - done)

        @pl.loop(0, (most + 7) // 8)
        def _(number):
            add_up(split(pick(sub + done + number * 8), 8), False)

    section(0, True)
    if blocks > span:
        pl.loop(1, blocks // span)(lambda s: section(s * span, False))
    both = 2 * TILE_V
    result = total_ref[0:both, :]
    for i in range(1, SUPPORT):
        result = result + pltpu.roll(total_ref[i * both : (i + 1) * both, :], i, axis=1)
    out_ref[0] = result[:TILE_V]
    out_ref[1] = result[TILE_V:]


def table_of(kernel_table):
    kernels = kernel_table.shape[0]
    return kernel_table.reshape(kernels // 256, 256, 2 * AREA).transpose(0, 2, 1).reshape(-1, 256)


def grid(arrived, table, chans):
    rows = arrived.reshape(-1, LANES)
    blocks = rows.shape[0] // 8
    span = 32 if blocks % 32 == 0 else blocks
    width = GRID_U // chans
    return pl.pallas_call(
        functools.partial(grid_kernel, span),
        out_shape=jax.ShapeDtypeStruct((2, TILE_V, width), jnp.float32),
        in_specs=[pl.BlockSpec(memory_space=pltpu.VMEM)] * 2,
        out_specs=pl.BlockSpec(memory_space=pltpu.VMEM),
        scratch_shapes=[pltpu.VMEM((2 * TILE_V * SUPPORT, width), jnp.float32)],
        compiler_params=pltpu.CompilerParams(vmem_limit_bytes=32 * 1024 * 1024),
    )(rows, table)


def body(visibility, kernel_table, cell_index, tile_index, plane_index, offset_index):
    chans, tiles = lax.axis_size("chan"), lax.axis_size("tile")
    packed = pack(chans * tiles, visibility, cell_index, tile_index[:, 0], plane_index, offset_index)
    first = (chans - 1) // 2 * 2 * tiles + tiles - 1
    order = [first] + [c * tiles + t for t in range(tiles) for c in range(chans) if c * tiles + t != first]
    arrived = lax.all_to_all(
        packed, ("chan", "tile"), split_axis=0, concat_axis=0, axis_index_groups=[order]
    )
    return grid(arrived, table_of(kernel_table), chans)


def solution(mesh):
    placed = (
        P(None, ("chan", "tile")),
        P(),
        P(("chan", "tile")),
        P(("chan", "tile"), None),
        P(("chan", "tile")),
        P(("chan", "tile")),
    )
    return jax.shard_map(
        body, mesh=mesh, in_specs=placed, out_specs=P(None, "tile", "chan"), check_vma=False
    )
```

```python
import functools

import jax
import jax.numpy as jnp
from jax import lax
from jax.experimental import pallas as pl
from jax.experimental.pallas import tpu as pltpu
from jax.sharding import PartitionSpec as P

GRID_U = 4096
SUPPORT = 8
OVERSAMPLE = 8
TILE_V = 16
AREA = SUPPORT * SUPPORT
LANES = 128
BLOCK = 2 * LANES
PLAIN = 4
PIECE = 256


def pack_kernel(*refs):
    far, out_ref, near, sems = refs[:5], refs[6], refs[7:12], refs[12]
    copies = [pltpu.make_async_copy(a, b, sems.at[i]) for i, (a, b) in enumerate(zip(far, near))]
    for copy in copies:
        copy.start()
    for copy in copies:
        copy.wait()
    vis_ref, cell_ref, tile_ref, plane_ref, offset_ref = near
    rows = vis_ref.shape[1]
    address = (tile_ref[...] * (TILE_V * GRID_U) + cell_ref[...]).astype(jnp.float32)
    kind = (plane_ref[...] * (OVERSAMPLE * OVERSAMPLE) + offset_ref[...]).astype(jnp.float32)
    parts = []
    for first in range(0, rows, BLOCK):
        for q in range(2):
            for half in range(2):
                start = first + half * LANES
                parts.append(vis_ref[q : q + 1, start : start + LANES])
        at = first // LANES
        parts.append(address[at : at + 2])
        parts.append(kind[at : at + 2])
    packed = jnp.concatenate(parts, axis=0)

    for d in range(out_ref.shape[0]):
        out_ref[d] = packed


def pack(devices, visibility, cell, tile, plane, offset, table):
    rows = visibility.shape[1]
    flat = [a.reshape(rows // LANES, LANES) for a in (cell, tile, plane, offset)]
    operands = (visibility, *flat)
    return pl.pallas_call(
        pack_kernel,
        out_shape=jax.ShapeDtypeStruct((devices, rows // BLOCK * 8, LANES), jnp.float32),
        in_specs=[pl.BlockSpec(memory_space=pltpu.HBM)] * 6,
        out_specs=pl.BlockSpec(memory_space=pltpu.VMEM),
        scratch_shapes=[pltpu.VMEM(a.shape, a.dtype) for a in operands]
        + [pltpu.SemaphoreType.DMA((len(operands),))],
        compiler_params=pltpu.CompilerParams(vmem_limit_bytes=4 * 1024 * 1024),
    )(*[pltpu.with_memory_space_constraint(a, pltpu.HBM) for a in (*operands, table)])


def along_lanes(values, index):
    return jnp.take_along_axis(values, index, axis=1, mode="promise_in_bounds")


def along_sublanes(values, index):
    return jnp.take_along_axis(values, index, axis=0, mode="promise_in_bounds")


def iota(shape, axis):
    return lax.broadcasted_iota(jnp.int32, shape, axis)


def dot(a, b, dims):
    return lax.dot_general(a, b, (dims, ((), ())), preferred_element_type=jnp.float32)


def ranks_down(marks):
    sub = iota((8, LANES), 0)
    above = jnp.zeros((8, LANES), jnp.int32)
    ranks = []
    for tile in marks:
        run = tile
        for by in (1, 2, 4):
            run = run + jnp.where(sub >= by, pltpu.roll(run, by, axis=0), 0)
        ranks.append(above + run - tile)
        above = above + jnp.broadcast_to(run[7:8], run.shape)
    return ranks, above


def grid_kernel(span, rows_ref, table_ref, out_ref, total_ref):
    width = out_ref.shape[2]
    blocks = rows_ref.shape[0] // 8
    first_u = lax.axis_index("chan") * width
    first_v = lax.axis_index("tile") * TILE_V
    sub = iota((8, LANES), 0)

    turned_table = [table_ref[k : k + 256, :].T for k in range(0, table_ref.shape[0], 256)]

    def section(first_block, fresh):
        def column(q, first):
            return rows_ref[pl.ds(first_block * 8 + first * 8 + q, 8, stride=8), :]

        real, imag, code, marks = [], [], [], []
        for half in range(2):
            for first in range(0, span, 8):
                real.append(column(half, first))
                imag.append(column(2 + half, first))
                address = column(4 + half, first).astype(jnp.int32)
                kind = column(6 + half, first).astype(jnp.int32)
                v_rel = (address >> 12) - first_v
                u_rel = (address & (GRID_U - 1)) - first_u
                touches = (v_rel > -SUPPORT) & (v_rel < TILE_V) & (u_rel > -SUPPORT) & (u_rel < width)
                marks.append(jnp.where(touches, 1, 0))
                code.append(kind + ((u_rel + SUPPORT) << 11) + ((v_rel + SUPPORT) << 24))
        ranks, total = ranks_down(marks)
        ranks = [jnp.where(m > 0, r, -1) for m, r in zip(marks, ranks)]
        lines = [[jnp.broadcast_to(r[j : j + 1], r.shape) for j in range(8)] for r in ranks]

        def pick(wanted):
            got = [jnp.zeros((8, LANES), x[0].dtype) for x in (real, imag, code)]
            for k, line in enumerate(lines):
                source = jnp.full((8, LANES), -1, jnp.int32)
                for j in range(8):
                    source = jnp.where(line[j] == wanted, j, source)
                for q, x in enumerate((real, imag, code)):
                    got[q] = jnp.where(source >= 0, along_sublanes(x[k], source & 7), got[q])
            return got

        def split(tiles, count):
            return [[tiles[q][r : r + 1] for r in range(count)] for q in range(3)]

        def add_up(lists, fresh):
            spreads, places = [], []
            for first in range(0, len(lists[0]), PIECE // LANES):
                vr, vi, code_n = [jnp.concatenate(l[first : first + PIECE // LANES], axis=1) for l in lists]
                kind_n = code_n & 2047
                u_n = ((code_n >> 11) & 8191) - SUPPORT
                v_n = (code_n >> 24) - SUPPORT
                low = kind_n & 255
                high = kind_n >> 8
                onehot = jnp.where(iota((256, PIECE), 0) == low, 1.0, 0.0).astype(jnp.bfloat16)
                kern = jnp.zeros((2 * AREA, PIECE), jnp.float32)
                for t in range(table_ref.shape[0] // 256):
                    part = dot(turned_table[t], onehot, ((1,), (0,)))
                    kern = jnp.where(high == t, part, kern)
                real_kern = kern[:AREA]
                imag_kern = kern[AREA:]
                weighted = (vr * real_kern - vi * imag_kern, vr * imag_kern + vi * real_kern)
                sub_n = iota((SUPPORT, PIECE), 0)
                turn = (sub_n - v_n) & (SUPPORT - 1)
                inside = [(sub_n + 8 * y >= v_n) & (sub_n + 8 * y < v_n + SUPPORT) for y in range(2)]
                spread = []
                for i in range(SUPPORT):
                    in_u = (u_n + i >= 0) & (u_n + i < width)
                    for c in range(2):
                        turned = along_sublanes(weighted[c][i * 8 : (i + 1) * 8], turn)
                        for y in range(2):
                            spread.append(jnp.where(inside[y] & in_u, turned, 0.0))
                spreads.append(jnp.concatenate(spread, axis=0).astype(jnp.bfloat16))
                column_n = jnp.where(u_n < 0, u_n + width, u_n)
                places.append(jnp.where(iota((width, PIECE), 0) == column_n, 1.0, 0.0).astype(jnp.bfloat16))
            sums = dot(jnp.concatenate(spreads, axis=1), jnp.concatenate(places, axis=1), ((1,), (1,)))
            if fresh:
                total_ref[...] = sums
            else:
                total_ref[...] += sums

        beyond = jnp.maximum(total - PLAIN, 0)
        lane = iota((LANES, LANES), 0)
        other = iota((LANES, LANES), 1)
        left = jnp.where(((lane & 15) == (other & 15)) & (lane < other), 1.0, 0.0).astype(jnp.bfloat16)
        skip = dot(beyond.astype(jnp.float32).astype(jnp.bfloat16), left, ((1,), (0,))).astype(jnp.int32)
        lists = split(pick(sub), PLAIN)
        group = iota((8, LANES), 1) >> 4
        for first in (0, 8):
            wanted = sub + first - skip
            shared = pick(jnp.where(wanted >= 0, wanted + PLAIN, -2))
            for q, x in enumerate(shared):
                for by in (16, 32, 64):
                    x = x + pltpu.roll(x, by, axis=1)
                x = jnp.where(group == sub, x, jnp.zeros_like(x))
                for by in (1, 2, 4):
                    x = x + pltpu.roll(x, by, axis=0)
                lists[q].append(x[0:1])
        add_up(lists, fresh)
        done = PLAIN + jnp.maximum(16 - skip, 0)
        most = jnp.max(total - done)

        @pl.loop(0, (most + 7) // 8)
        def _(number):
            add_up(split(pick(sub + done + number * 8), 8), False)

    section(0, True)
    if blocks > span:
        pl.loop(1, blocks // span)(lambda s: section(s * span, False))
    both = 2 * TILE_V
    result = total_ref[0:both, :]
    for i in range(1, SUPPORT):
        result = result + pltpu.roll(total_ref[i * both : (i + 1) * both, :], i, axis=1)
    out_ref[0] = result[:TILE_V]
    out_ref[1] = result[TILE_V:]


def table_of(kernel_table):
    return kernel_table


def grid(arrived, table, chans):
    rows = arrived.reshape(-1, LANES)
    blocks = rows.shape[0] // 8
    span = 32 if blocks % 32 == 0 else blocks
    width = GRID_U // chans
    return pl.pallas_call(
        functools.partial(grid_kernel, span),
        out_shape=jax.ShapeDtypeStruct((2, TILE_V, width), jnp.float32),
        in_specs=[pl.BlockSpec(memory_space=pltpu.VMEM)] * 2,
        out_specs=pl.BlockSpec(memory_space=pltpu.VMEM),
        scratch_shapes=[pltpu.VMEM((2 * TILE_V * SUPPORT, width), jnp.float32)],
        compiler_params=pltpu.CompilerParams(vmem_limit_bytes=32 * 1024 * 1024),
    )(rows, table)


def body(visibility, kernel_table, cell_index, tile_index, plane_index, offset_index):
    chans, tiles = lax.axis_size("chan"), lax.axis_size("tile")
    packed = pack(chans * tiles, visibility, cell_index, tile_index[:, 0], plane_index, offset_index, kernel_table)
    first = (chans - 1) // 2 * 2 * tiles + tiles - 1
    order = [first] + [c * tiles + t for t in range(tiles) for c in range(chans) if c * tiles + t != first]
    arrived = lax.all_to_all(
        packed, ("chan", "tile"), split_axis=0, concat_axis=0, axis_index_groups=[order]
    )
    return grid(arrived, table_of(kernel_table), chans)


def solution(mesh):
    placed = (
        P(None, ("chan", "tile")),
        P(),
        P(("chan", "tile")),
        P(("chan", "tile"), None),
        P(("chan", "tile")),
        P(("chan", "tile")),
    )
    return jax.shard_map(
        body, mesh=mesh, in_specs=placed, out_specs=P(None, "tile", "chan"), check_vma=False
    )
```

```python
import functools
import itertools

import jax
import jax.numpy as jnp
from jax import lax
from jax.experimental import pallas as pl
from jax.experimental.pallas import tpu as pltpu
from jax.sharding import PartitionSpec as P

GRID_U = 4096
SUPPORT = 8
OVERSAMPLE = 8
TILE_V = 16
AREA = SUPPORT * SUPPORT
LANES = 128
BLOCK = 2 * LANES
PLAIN = 4
PIECE = 256


def pack_kernel(*refs):
    far, out_ref, near, sems = refs[:5], refs[6], refs[7:12], refs[12]
    copies = [pltpu.make_async_copy(a, b, sems.at[i]) for i, (a, b) in enumerate(zip(far, near))]
    for copy in copies:
        copy.start()
    for copy in copies:
        copy.wait()
    vis_ref, cell_ref, tile_ref, plane_ref, offset_ref = near
    rows = vis_ref.shape[1]
    address = (tile_ref[...] * (TILE_V * GRID_U) + cell_ref[...]).astype(jnp.float32)
    kind = (plane_ref[...] * (OVERSAMPLE * OVERSAMPLE) + offset_ref[...]).astype(jnp.float32)
    parts = []
    for first in range(0, rows, BLOCK):
        for q in range(2):
            for half in range(2):
                start = first + half * LANES
                parts.append(vis_ref[q : q + 1, start : start + LANES])
        at = first // LANES
        parts.append(address[at : at + 2])
        parts.append(kind[at : at + 2])
    packed = jnp.concatenate(parts, axis=0)

    for d in range(out_ref.shape[0]):
        out_ref[d] = packed


def pack(devices, visibility, cell, tile, plane, offset, table):
    rows = visibility.shape[1]
    flat = [a.reshape(rows // LANES, LANES) for a in (cell, tile, plane, offset)]
    operands = (visibility, *flat)
    return pl.pallas_call(
        pack_kernel,
        out_shape=jax.ShapeDtypeStruct((devices, rows // BLOCK * 8, LANES), jnp.float32),
        in_specs=[pl.BlockSpec(memory_space=pltpu.HBM)] * 6,
        out_specs=pl.BlockSpec(memory_space=pltpu.VMEM),
        scratch_shapes=[pltpu.VMEM(a.shape, a.dtype) for a in operands]
        + [pltpu.SemaphoreType.DMA((len(operands),))],
        compiler_params=pltpu.CompilerParams(vmem_limit_bytes=4 * 1024 * 1024),
    )(*[pltpu.with_memory_space_constraint(a, pltpu.HBM) for a in (*operands, table)])


def along_lanes(values, index):
    return jnp.take_along_axis(values, index, axis=1, mode="promise_in_bounds")


def along_sublanes(values, index):
    return jnp.take_along_axis(values, index, axis=0, mode="promise_in_bounds")


def iota(shape, axis):
    return lax.broadcasted_iota(jnp.int32, shape, axis)


def dot(a, b, dims):
    return lax.dot_general(a, b, (dims, ((), ())), preferred_element_type=jnp.float32)


def ranks_down(marks):
    sub = iota((8, LANES), 0)
    above = jnp.zeros((8, LANES), jnp.int32)
    ranks = []
    for tile in marks:
        run = tile
        for by in (1, 2, 4):
            run = run + jnp.where(sub >= by, pltpu.roll(run, by, axis=0), 0)
        ranks.append(above + run - tile)
        above = above + jnp.broadcast_to(run[7:8], run.shape)
    return ranks, above


def grid_kernel(span, own_ref, other_ref, table_ref, out_ref, total_ref):
    width = out_ref.shape[2]
    blocks = own_ref.shape[0] // 8
    first_u = lax.axis_index("chan") * width
    first_v = lax.axis_index("tile") * TILE_V
    sub = iota((8, LANES), 0)

    turned_table = [table_ref[k : k + 256, :].T for k in range(0, table_ref.shape[0], 256)]

    def section(first_block, fresh):
        def column(ref, q, first):
            return ref[pl.ds(first_block * 8 + first * 8 + q, 8, stride=8), :]

        real, imag, code, marks = [], [], [], []
        for ref, half, first in itertools.product((own_ref, other_ref), range(2), range(0, span, 8)):
            real.append(column(ref, half, first))
            imag.append(column(ref, 2 + half, first))
            address = column(ref, 4 + half, first).astype(jnp.int32)
            kind = column(ref, 6 + half, first).astype(jnp.int32)
            v_rel = (address >> 12) - first_v
            u_rel = (address & (GRID_U - 1)) - first_u
            touches = (v_rel > -SUPPORT) & (v_rel < TILE_V) & (u_rel > -SUPPORT) & (u_rel < width)
            marks.append(jnp.where(touches, 1, 0))
            code.append(kind + ((u_rel + SUPPORT) << 11) + ((v_rel + SUPPORT) << 24))
        ranks, total = ranks_down(marks)
        ranks = [jnp.where(m > 0, r, -1) for m, r in zip(marks, ranks)]
        lines = [[jnp.broadcast_to(r[j : j + 1], r.shape) for j in range(8)] for r in ranks]

        def pick(wanted):
            got = [jnp.zeros((8, LANES), x[0].dtype) for x in (real, imag, code)]
            for k, line in enumerate(lines):
                source = jnp.full((8, LANES), -1, jnp.int32)
                for j in range(8):
                    source = jnp.where(line[j] == wanted, j, source)
                for q, x in enumerate((real, imag, code)):
                    got[q] = jnp.where(source >= 0, along_sublanes(x[k], source & 7), got[q])
            return got

        def split(tiles, count):
            return [[tiles[q][r : r + 1] for r in range(count)] for q in range(3)]

        def add_up(lists, fresh):
            spreads, places = [], []
            for first in range(0, len(lists[0]), PIECE // LANES):
                vr, vi, code_n = [jnp.concatenate(l[first : first + PIECE // LANES], axis=1) for l in lists]
                kind_n = code_n & 2047
                u_n = ((code_n >> 11) & 8191) - SUPPORT
                v_n = (code_n >> 24) - SUPPORT
                low = kind_n & 255
                high = kind_n >> 8
                onehot = jnp.where(iota((256, PIECE), 0) == low, 1.0, 0.0).astype(jnp.bfloat16)
                kern = jnp.zeros((2 * AREA, PIECE), jnp.float32)
                for t in range(table_ref.shape[0] // 256):
                    part = dot(turned_table[t], onehot, ((1,), (0,)))
                    kern = jnp.where(high == t, part, kern)
                real_kern = kern[:AREA]
                imag_kern = kern[AREA:]
                weighted = (vr * real_kern - vi * imag_kern, vr * imag_kern + vi * real_kern)
                sub_n = iota((SUPPORT, PIECE), 0)
                turn = (sub_n - v_n) & (SUPPORT - 1)
                inside = [(sub_n + 8 * y >= v_n) & (sub_n + 8 * y < v_n + SUPPORT) for y in range(2)]
                spread = []
                for i in range(SUPPORT):
                    in_u = (u_n + i >= 0) & (u_n + i < width)
                    for c in range(2):
                        turned = along_sublanes(weighted[c][i * 8 : (i + 1) * 8], turn)
                        for y in range(2):
                            spread.append(jnp.where(inside[y] & in_u, turned, 0.0))
                spreads.append(jnp.concatenate(spread, axis=0).astype(jnp.bfloat16))
                column_n = jnp.where(u_n < 0, u_n + width, u_n)
                places.append(jnp.where(iota((width, PIECE), 0) == column_n, 1.0, 0.0).astype(jnp.bfloat16))
            sums = dot(jnp.concatenate(spreads, axis=1), jnp.concatenate(places, axis=1), ((1,), (1,)))
            if fresh:
                total_ref[...] = sums
            else:
                total_ref[...] += sums

        beyond = jnp.maximum(total - PLAIN, 0)
        lane = iota((LANES, LANES), 0)
        other = iota((LANES, LANES), 1)
        left = jnp.where(((lane & 15) == (other & 15)) & (lane < other), 1.0, 0.0).astype(jnp.bfloat16)
        skip = dot(beyond.astype(jnp.float32).astype(jnp.bfloat16), left, ((1,), (0,))).astype(jnp.int32)
        lists = split(pick(sub), PLAIN)
        group = iota((8, LANES), 1) >> 4
        for first in (0, 8):
            wanted = sub + first - skip
            shared = pick(jnp.where(wanted >= 0, wanted + PLAIN, -2))
            for q, x in enumerate(shared):
                for by in (16, 32, 64):
                    x = x + pltpu.roll(x, by, axis=1)
                x = jnp.where(group == sub, x, jnp.zeros_like(x))
                for by in (1, 2, 4):
                    x = x + pltpu.roll(x, by, axis=0)
                lists[q].append(x[0:1])
        add_up(lists, fresh)
        done = PLAIN + jnp.maximum(16 - skip, 0)
        most = jnp.max(total - done)

        @pl.loop(0, (most + 7) // 8)
        def _(number):
            add_up(split(pick(sub + done + number * 8), 8), False)

    section(0, True)
    if blocks > span:
        pl.loop(1, blocks // span)(lambda s: section(s * span, False))
    both = 2 * TILE_V
    result = total_ref[0:both, :]
    for i in range(1, SUPPORT):
        result = result + pltpu.roll(total_ref[i * both : (i + 1) * both, :], i, axis=1)
    out_ref[0] = result[:TILE_V]
    out_ref[1] = result[TILE_V:]


def table_of(kernel_table):
    return kernel_table


def grid(arrived, table, chans):
    rows = [part.reshape(-1, LANES) for part in arrived]
    blocks = rows[0].shape[0] // 8
    span = 16 if blocks % 16 == 0 else blocks
    width = GRID_U // chans
    return pl.pallas_call(
        functools.partial(grid_kernel, span),
        out_shape=jax.ShapeDtypeStruct((2, TILE_V, width), jnp.float32),
        in_specs=[pl.BlockSpec(memory_space=pltpu.VMEM)] * 3,
        out_specs=pl.BlockSpec(memory_space=pltpu.VMEM),
        scratch_shapes=[pltpu.VMEM((2 * TILE_V * SUPPORT, width), jnp.float32)],
        compiler_params=pltpu.CompilerParams(vmem_limit_bytes=32 * 1024 * 1024),
    )(*rows, table)


def body(visibility, kernel_table, cell_index, tile_index, plane_index, offset_index):
    chans, tiles = lax.axis_size("chan"), lax.axis_size("tile")
    packed = pack(chans // 2 * tiles, visibility, cell_index, tile_index[:, 0], plane_index, offset_index, kernel_table)
    chips = [(c, t) for t in range(tiles) for c in range(0, chans, 2)][::-1]
    groups = [[(c + (side ^ (2 * t >= tiles))) * tiles + t for c, t in chips] for side in range(2)]
    arrived = lax.all_to_all(
        packed, ("chan", "tile"), split_axis=0, concat_axis=0, axis_index_groups=groups
    )
    swapped = lax.ppermute(arrived, "chan", [(c, c ^ 1) for c in range(chans)])
    return grid((arrived, swapped), table_of(kernel_table), chans)


def solution(mesh):
    placed = (
        P(None, ("chan", "tile")),
        P(),
        P(("chan", "tile")),
        P(("chan", "tile"), None),
        P(("chan", "tile")),
        P(("chan", "tile")),
    )
    return jax.shard_map(
        body, mesh=mesh, in_specs=placed, out_specs=P(None, "tile", "chan"), check_vma=False
    )
```

```python
import functools

import jax
import jax.numpy as jnp
from jax import lax
from jax.experimental import pallas as pl
from jax.experimental.pallas import tpu as pltpu
from jax.sharding import PartitionSpec as P

GRID_U = 4096
SUPPORT = 8
OVERSAMPLE = 8
TILE_V = 16
AREA = SUPPORT * SUPPORT
LANES = 128
BLOCK = 2 * LANES
PLAIN = 1
DEEP = 6
FIRST_SHARE = 16
SECOND_SHARE = 32
PIECE = 256


def pack_kernel(*refs):
    far, out_ref, near, sems = refs[:5], refs[6], refs[7:12], refs[12]
    copies = [pltpu.make_async_copy(a, b, sems.at[i]) for i, (a, b) in enumerate(zip(far, near))]
    for copy in copies:
        copy.start()
    for copy in copies:
        copy.wait()
    vis_ref, cell_ref, tile_ref, plane_ref, offset_ref = near
    rows = vis_ref.shape[1]
    address = (tile_ref[...] * (TILE_V * GRID_U) + cell_ref[...]).astype(jnp.float32)
    kind = (plane_ref[...] * (OVERSAMPLE * OVERSAMPLE) + offset_ref[...]).astype(jnp.float32)
    parts = []
    for first in range(0, rows, BLOCK):
        for q in range(2):
            for half in range(2):
                start = first + half * LANES
                parts.append(vis_ref[q : q + 1, start : start + LANES])
        at = first // LANES
        parts.append(address[at : at + 2])
        parts.append(kind[at : at + 2])
    packed = jnp.concatenate(parts, axis=0)

    for d in range(out_ref.shape[0]):
        out_ref[d] = packed


def pack(devices, visibility, cell, tile, plane, offset, table):
    rows = visibility.shape[1]
    flat = [a.reshape(rows // LANES, LANES) for a in (cell, tile, plane, offset)]
    operands = (visibility, *flat)
    return pl.pallas_call(
        pack_kernel,
        out_shape=jax.ShapeDtypeStruct((devices, rows // BLOCK * 8, LANES), jnp.float32),
        in_specs=[pl.BlockSpec(memory_space=pltpu.HBM)] * 6,
        out_specs=pl.BlockSpec(memory_space=pltpu.VMEM),
        scratch_shapes=[pltpu.VMEM(a.shape, a.dtype) for a in operands]
        + [pltpu.SemaphoreType.DMA((len(operands),))],
        compiler_params=pltpu.CompilerParams(vmem_limit_bytes=4 * 1024 * 1024),
    )(*[pltpu.with_memory_space_constraint(a, pltpu.HBM) for a in (*operands, table)])


def along_lanes(values, index):
    return jnp.take_along_axis(values, index, axis=1, mode="promise_in_bounds")


def along_sublanes(values, index):
    return jnp.take_along_axis(values, index, axis=0, mode="promise_in_bounds")


def iota(shape, axis):
    return lax.broadcasted_iota(jnp.int32, shape, axis)


def dot(a, b, dims):
    return lax.dot_general(a, b, (dims, ((), ())), preferred_element_type=jnp.float32)


class Gridder:
    def __init__(self, width, table_ref):
        self.width = width
        self.first_u = lax.axis_index("chan") * width
        self.first_v = lax.axis_index("tile") * TILE_V
        self.half = iota((8, LANES), 0) & 1
        self.rows_b = iota((256, PIECE), 0).astype(jnp.float32).astype(jnp.bfloat16)
        self.table = [table_ref[k : k + 256, :].T for k in range(0, table_ref.shape[0], 256)]

    def line(self, values):
        return jnp.broadcast_to(values.astype(jnp.float32).astype(jnp.bfloat16), (256, PIECE))

    def sums(self, tiles):
        width, one, zero = self.width, jnp.bfloat16(1), jnp.bfloat16(0)
        spreads, places = [], []
        for tile in tiles:
            vr, vi, address, kind = [
                jnp.concatenate([tile[2 * q : 2 * q + 1], tile[2 * q + 1 : 2 * q + 2]], axis=1) for q in range(4)
            ]
            address = address.astype(jnp.int32)
            kind = kind.astype(jnp.int32)
            u_n = (address & (GRID_U - 1)) - self.first_u
            v_n = (address >> 12) - self.first_v
            high = kind >> 8
            onehot = jnp.where(self.rows_b == self.line(kind & 255), one, zero)
            kern = jnp.zeros((2 * AREA, PIECE), jnp.float32)
            for k, part in enumerate(self.table):
                kern = jnp.where(high == k, dot(part, onehot, ((1,), (0,))), kern)
            real_kern = kern[:AREA]
            imag_kern = kern[AREA:]
            weighted = (vr * real_kern - vi * imag_kern, vr * imag_kern + vi * real_kern)
            sub = iota((SUPPORT, PIECE), 0)
            turn = (sub - v_n) & (SUPPORT - 1)
            inside = [(sub + 8 * y >= v_n) & (sub + 8 * y < v_n + SUPPORT) for y in range(2)]
            spread = []
            for i in range(SUPPORT):
                in_u = (u_n + i >= 0) & (u_n + i < width)
                for c in range(2):
                    turned = along_sublanes(weighted[c][i * 8 : (i + 1) * 8], turn)
                    for y in range(2):
                        spread.append(jnp.where(inside[y] & in_u, turned, 0.0))
            spreads.append(jnp.concatenate(spread, axis=0).astype(jnp.bfloat16))
            column = jnp.where(u_n < 0, u_n + width, u_n)
            near = jnp.where(self.rows_b == self.line(column & 255), one, zero)
            far = self.line(column >> 8)
            place = [jnp.where(far == h, near, zero) for h in range(-(-width // 256))]
            places.append(jnp.concatenate(place, axis=0)[:width])
        return dot(jnp.concatenate(spreads, axis=1), jnp.concatenate(places, axis=1), ((1,), (1,)))

    def marked(self, rows_ref, first_block, span):
        tiles, ranks = [], []
        total = jnp.zeros((8, LANES), jnp.int32)
        for block in range(span):
            tile = rows_ref[pl.ds((first_block + block) * 8, 8), :]
            address = tile.astype(jnp.int32)
            v_rel = (address >> 12) - self.first_v
            u_rel = (address & (GRID_U - 1)) - self.first_u
            touches = (v_rel > -SUPPORT) & (v_rel < TILE_V) & (u_rel > -SUPPORT) & (u_rel < self.width)
            here = along_sublanes(jnp.where(touches, 1, 0), 4 + self.half)
            ranks.append(jnp.where(here > 0, total, -1))
            tiles.append(tile)
            total = total + here
        return tiles, ranks, total

    def later_sections(self, rows_ref, span, sums_ref):
        blocks = rows_ref.shape[0] // 8
        if blocks > span:

            @pl.loop(1, blocks // span)
            def _(section):
                tiles, ranks, total = self.marked(rows_ref, section * span, span)

                @pl.loop(0, (jnp.max(total) + 1) // 2)
                def _(pair):
                    sums_ref[...] += self.sums([ranked(tiles, ranks, 2 * pair + e) for e in range(2)])


def ranked(tiles, ranks, wanted):
    got = jnp.zeros((8, LANES), jnp.float32)
    for tile, rank in zip(tiles, ranks):
        got = jnp.where(rank == wanted, tile, got)
    return got


def add_rows(grid, share, span, rows_ref, sums_ref, first):
    sub, lane = iota((8, LANES), 0), iota((8, LANES), 1)
    half = grid.half
    tiles, ranks, total = grid.marked(rows_ref, 0, span)
    beyond = jnp.maximum(total - PLAIN, 0)
    skip = jnp.zeros_like(beyond)
    every = beyond
    for by in range(share, LANES, share):
        earlier = pltpu.roll(beyond, by, axis=1)
        skip = skip + jnp.where(lane >= by, earlier, 0)
        every = every + earlier
    skip = skip + jnp.where(half > 0, along_sublanes(every, sub ^ 1), 0)
    plain = [ranked(tiles, ranks, r) for r in range(PLAIN)]
    more = [ranked(tiles, ranks, r) for r in range(PLAIN, DEEP)]
    slots = 2 * LANES // share
    moved = []
    for slot in range(slots):
        got = jnp.zeros((8, LANES), jnp.float32)
        for k, tile in enumerate(more):
            got = jnp.where(skip == slot - k, tile, got)
        moved.append(got)
    folded = []
    for even, odd in zip(moved[::2], moved[1::2]):
        folded.append(jnp.where(half == 0, even, odd) + along_sublanes(jnp.where(half == 0, odd, even), sub ^ 1))
    by = LANES // 2
    while by >= share:
        count = len(folded) // 2
        upper = (lane & by) > 0
        folded = [
            jnp.where(upper, folded[k + count], folded[k])
            + along_lanes(jnp.where(upper, folded[k], folded[k + count]), lane ^ by)
            for k in range(count)
        ]
        by //= 2
    sums_ref[...] = first(grid.sums([*plain, *folded]))
    done = jnp.clip(PLAIN + slots - skip, PLAIN, DEEP)

    @pl.loop(0, (jnp.max(total - done) + 1) // 2)
    def _(pair):
        sums_ref[...] += grid.sums([ranked(tiles, ranks, done + (2 * pair + e)) for e in range(2)])

    grid.later_sections(rows_ref, span, sums_ref)


def first_kernel(span, rows_ref, table_ref, sums_ref):
    add_rows(Gridder(sums_ref.shape[1], table_ref), FIRST_SHARE, span, rows_ref, sums_ref, lambda sums: sums)


def second_kernel(span, rows_ref, table_ref, begun_ref, out_ref, sums_ref):
    grid = Gridder(out_ref.shape[2], table_ref)
    add_rows(grid, SECOND_SHARE, span, rows_ref, sums_ref, lambda sums: begun_ref[...] + sums)
    both = 2 * TILE_V
    result = sums_ref[0:both, :]
    for i in range(1, SUPPORT):
        result = result + pltpu.roll(sums_ref[i * both : (i + 1) * both, :], i, axis=1)
    out_ref[0] = result[:TILE_V]
    out_ref[1] = result[TILE_V:]


def grid(own, other, table, chans):
    own, other = [part.reshape(-1, LANES) for part in (own, other)]
    blocks = own.shape[0] // 8
    span = 16 if blocks % 16 == 0 else blocks
    width = GRID_U // chans
    taps = 2 * TILE_V * SUPPORT
    vmem = pl.BlockSpec(memory_space=pltpu.VMEM)
    params = pltpu.CompilerParams(vmem_limit_bytes=16 * 1024 * 1024)
    cost = pl.CostEstimate(flops=10**9, bytes_accessed=10**6, transcendentals=0)
    begun = pl.pallas_call(
        functools.partial(first_kernel, span),
        out_shape=pltpu.VMEM((taps, width), jnp.float32),
        in_specs=[vmem] * 2,
        out_specs=vmem,
        compiler_params=params,
        cost_estimate=cost,
    )(own, table)
    return pl.pallas_call(
        functools.partial(second_kernel, span),
        out_shape=jax.ShapeDtypeStruct((2, TILE_V, width), jnp.float32),
        in_specs=[vmem] * 3,
        out_specs=vmem,
        scratch_shapes=[pltpu.VMEM((taps, width), jnp.float32)],
        compiler_params=params,
        cost_estimate=cost,
    )(other, table, begun)


def body(visibility, kernel_table, cell_index, tile_index, plane_index, offset_index):
    chans, tiles = lax.axis_size("chan"), lax.axis_size("tile")
    packed = pack(chans // 2 * tiles, visibility, cell_index, tile_index[:, 0], plane_index, offset_index, kernel_table)
    chips = [(c, t) for t in range(tiles) for c in range(0, chans, 2)][::-1]
    chips.insert(0, chips.pop(chans // 2))
    groups = [[(c + (side ^ (4 * t >= 3 * tiles))) * tiles + t for c, t in chips] for side in range(2)]
    arrived = lax.all_to_all(
        packed, ("chan", "tile"), split_axis=0, concat_axis=0, axis_index_groups=groups
    )
    swapped = lax.ppermute(arrived, "chan", [(c, c ^ 1) for c in range(chans)])
    return grid(arrived, swapped, kernel_table, chans)


def solution(mesh):
    placed = (
        P(None, ("chan", "tile")),
        P(),
        P(("chan", "tile")),
        P(("chan", "tile"), None),
        P(("chan", "tile")),
        P(("chan", "tile")),
    )
    return jax.shard_map(
        body, mesh=mesh, in_specs=placed, out_specs=P(None, "tile", "chan"), check_vma=False
    )
```

```python
import functools

import jax
import jax.numpy as jnp
from jax import lax
from jax.experimental import pallas as pl
from jax.experimental.pallas import tpu as pltpu
from jax.sharding import PartitionSpec as P

GRID_U = 4096
SUPPORT = 8
OVERSAMPLE = 8
TILE_V = 16
AREA = SUPPORT * SUPPORT
LANES = 128
BLOCK = 2 * LANES
PLAIN = 1
DEEP = 6
SHARE = 32
PIECE = 256


def pack_kernel(*refs):
    far, out_ref, near, sems = refs[:5], refs[6], refs[7:12], refs[12]
    copies = [pltpu.make_async_copy(a, b, sems.at[i]) for i, (a, b) in enumerate(zip(far, near))]
    for copy in copies:
        copy.start()
    for copy in copies:
        copy.wait()
    vis_ref, cell_ref, tile_ref, plane_ref, offset_ref = near
    rows = vis_ref.shape[1]
    address = (tile_ref[...] * (TILE_V * GRID_U) + cell_ref[...]).astype(jnp.float32)
    kind = (plane_ref[...] * (OVERSAMPLE * OVERSAMPLE) + offset_ref[...]).astype(jnp.float32)
    parts = []
    for first in range(0, rows, BLOCK):
        for q in range(2):
            for half in range(2):
                start = first + half * LANES
                parts.append(vis_ref[q : q + 1, start : start + LANES])
        at = first // LANES
        parts.append(address[at : at + 2])
        parts.append(kind[at : at + 2])
    packed = jnp.concatenate(parts, axis=0)

    for d in range(out_ref.shape[0]):
        out_ref[d] = packed


def pack(devices, visibility, cell, tile, plane, offset, table):
    rows = visibility.shape[1]
    flat = [a.reshape(rows // LANES, LANES) for a in (cell, tile, plane, offset)]
    operands = (visibility, *flat)
    return pl.pallas_call(
        pack_kernel,
        out_shape=jax.ShapeDtypeStruct((devices, rows // BLOCK * 8, LANES), jnp.float32),
        in_specs=[pl.BlockSpec(memory_space=pltpu.HBM)] * 6,
        out_specs=pl.BlockSpec(memory_space=pltpu.VMEM),
        scratch_shapes=[pltpu.VMEM(a.shape, a.dtype) for a in operands]
        + [pltpu.SemaphoreType.DMA((len(operands),))],
        compiler_params=pltpu.CompilerParams(vmem_limit_bytes=4 * 1024 * 1024),
    )(*[pltpu.with_memory_space_constraint(a, pltpu.HBM) for a in (*operands, table)])


def along_lanes(values, index):
    return jnp.take_along_axis(values, index, axis=1, mode="promise_in_bounds")


def along_sublanes(values, index):
    return jnp.take_along_axis(values, index, axis=0, mode="promise_in_bounds")


def iota(shape, axis):
    return lax.broadcasted_iota(jnp.int32, shape, axis)


def dot(a, b, dims):
    return lax.dot_general(a, b, (dims, ((), ())), preferred_element_type=jnp.float32)


class Gridder:
    def __init__(self, width, table_ref):
        self.width = width
        self.first_u = lax.axis_index("chan") * width
        self.first_v = lax.axis_index("tile") * TILE_V
        self.half = iota((8, LANES), 0) & 1
        self.rows_b = iota((256, PIECE), 0).astype(jnp.float32).astype(jnp.bfloat16)
        self.table = [table_ref[k : k + 256, :].T for k in range(0, table_ref.shape[0], 256)]

    def line(self, values):
        return jnp.broadcast_to(values.astype(jnp.float32).astype(jnp.bfloat16), (256, PIECE))

    def sums(self, tiles):
        width, one, zero = self.width, jnp.bfloat16(1), jnp.bfloat16(0)
        spreads, places = [], []
        for tile in tiles:
            vr, vi, address, kind = [
                jnp.concatenate([tile[2 * q : 2 * q + 1], tile[2 * q + 1 : 2 * q + 2]], axis=1) for q in range(4)
            ]
            address = address.astype(jnp.int32)
            kind = kind.astype(jnp.int32)
            u_n = (address & (GRID_U - 1)) - self.first_u
            v_n = (address >> 12) - self.first_v
            high = kind >> 8
            onehot = jnp.where(self.rows_b == self.line(kind & 255), one, zero)
            kern = jnp.zeros((2 * AREA, PIECE), jnp.float32)
            for k, part in enumerate(self.table):
                kern = jnp.where(high == k, dot(part, onehot, ((1,), (0,))), kern)
            real_kern = kern[:AREA]
            imag_kern = kern[AREA:]
            weighted = (vr * real_kern - vi * imag_kern, vr * imag_kern + vi * real_kern)
            sub = iota((SUPPORT, PIECE), 0)
            turn = (sub - v_n) & (SUPPORT - 1)
            inside = [(sub + 8 * y >= v_n) & (sub + 8 * y < v_n + SUPPORT) for y in range(2)]
            spread = []
            for i in range(SUPPORT):
                in_u = (u_n + i >= 0) & (u_n + i < width)
                for c in range(2):
                    turned = along_sublanes(weighted[c][i * 8 : (i + 1) * 8], turn)
                    for y in range(2):
                        spread.append(jnp.where(inside[y] & in_u, turned, 0.0))
            spreads.append(jnp.concatenate(spread, axis=0).astype(jnp.bfloat16))
            column = jnp.where(u_n < 0, u_n + width, u_n)
            near = jnp.where(self.rows_b == self.line(column & 255), one, zero)
            far = self.line(column >> 8)
            place = [jnp.where(far == h, near, zero) for h in range(-(-width // 256))]
            places.append(jnp.concatenate(place, axis=0)[:width])
        return dot(jnp.concatenate(spreads, axis=1), jnp.concatenate(places, axis=1), ((1,), (1,)))

    def marked(self, rows_ref, first_block, span):
        tiles, ranks = [], []
        total = jnp.zeros((8, LANES), jnp.int32)
        for block in range(span):
            tile = rows_ref[pl.ds((first_block + block) * 8, 8), :]
            address = tile.astype(jnp.int32)
            v_rel = (address >> 12) - self.first_v
            u_rel = (address & (GRID_U - 1)) - self.first_u
            touches = (v_rel > -SUPPORT) & (v_rel < TILE_V) & (u_rel > -SUPPORT) & (u_rel < self.width)
            here = along_sublanes(jnp.where(touches, 1, 0), 4 + self.half)
            ranks.append(jnp.where(here > 0, total, -1))
            tiles.append(tile)
            total = total + here
        return tiles, ranks, total

    def later_sections(self, rows_ref, span, sums_ref):
        blocks = rows_ref.shape[0] // 8
        if blocks > span:

            @pl.loop(1, blocks // span)
            def _(section):
                tiles, ranks, total = self.marked(rows_ref, section * span, span)

                @pl.loop(0, (jnp.max(total) + 1) // 2)
                def _(pair):
                    sums_ref[...] += self.sums([ranked(tiles, ranks, 2 * pair + e) for e in range(2)])


def ranked(tiles, ranks, wanted):
    got = jnp.zeros((8, LANES), jnp.float32)
    for tile, rank in zip(tiles, ranks):
        got = jnp.where(rank == wanted, tile, got)
    return got


def add_rows(grid, span, rows_ref, sums_ref, first):
    sub, lane = iota((8, LANES), 0), iota((8, LANES), 1)
    half = grid.half
    tiles, ranks, total = grid.marked(rows_ref, 0, span)
    beyond = jnp.maximum(total - PLAIN, 0)
    skip = jnp.zeros_like(beyond)
    every = beyond
    for by in range(SHARE, LANES, SHARE):
        earlier = pltpu.roll(beyond, by, axis=1)
        skip = skip + jnp.where(lane >= by, earlier, 0)
        every = every + earlier
    skip = skip + jnp.where(half > 0, along_sublanes(every, sub ^ 1), 0)
    plain = [ranked(tiles, ranks, r) for r in range(PLAIN)]
    more = [ranked(tiles, ranks, r) for r in range(PLAIN, DEEP)]
    slots = 2 * LANES // SHARE
    moved = []
    for slot in range(slots):
        got = jnp.zeros((8, LANES), jnp.float32)
        for k, tile in enumerate(more):
            got = jnp.where(skip == slot - k, tile, got)
        moved.append(got)
    folded = []
    for even, odd in zip(moved[::2], moved[1::2]):
        folded.append(jnp.where(half == 0, even, odd) + along_sublanes(jnp.where(half == 0, odd, even), sub ^ 1))
    by = LANES // 2
    while by >= SHARE:
        count = len(folded) // 2
        upper = (lane & by) > 0
        folded = [
            jnp.where(upper, folded[k + count], folded[k])
            + along_lanes(jnp.where(upper, folded[k], folded[k + count]), lane ^ by)
            for k in range(count)
        ]
        by //= 2
    sums_ref[...] = first(grid.sums([*plain, *folded]))
    done = jnp.clip(PLAIN + slots - skip, PLAIN, DEEP)

    @pl.loop(0, jnp.max(total - done))
    def _(number):
        sums_ref[...] += grid.sums([ranked(tiles, ranks, done + number)])

    grid.later_sections(rows_ref, span, sums_ref)


def first_kernel(span, rows_ref, table_ref, sums_ref):
    add_rows(Gridder(sums_ref.shape[1], table_ref), span, rows_ref, sums_ref, lambda sums: sums)


def second_kernel(span, rows_ref, table_ref, begun_ref, out_ref, sums_ref):
    grid = Gridder(out_ref.shape[2], table_ref)
    add_rows(grid, span, rows_ref, sums_ref, lambda sums: begun_ref[...] + sums)
    both = 2 * TILE_V
    result = sums_ref[0:both, :]
    for i in range(1, SUPPORT):
        result = result + pltpu.roll(sums_ref[i * both : (i + 1) * both, :], i, axis=1)
    out_ref[0] = result[:TILE_V]
    out_ref[1] = result[TILE_V:]


def grid(own, other, table, chans):
    own, other = [part.reshape(-1, LANES) for part in (own, other)]
    blocks = own.shape[0] // 8
    span = 16 if blocks % 16 == 0 else blocks
    width = GRID_U // chans
    taps = 2 * TILE_V * SUPPORT
    vmem = pl.BlockSpec(memory_space=pltpu.VMEM)
    params = pltpu.CompilerParams(vmem_limit_bytes=16 * 1024 * 1024)
    cost = pl.CostEstimate(flops=10**9, bytes_accessed=10**6, transcendentals=0)
    begun = pl.pallas_call(
        functools.partial(first_kernel, span),
        out_shape=pltpu.VMEM((taps, width), jnp.float32),
        in_specs=[vmem] * 2,
        out_specs=vmem,
        compiler_params=params,
        cost_estimate=cost,
    )(own, table)
    return pl.pallas_call(
        functools.partial(second_kernel, span),
        out_shape=jax.ShapeDtypeStruct((2, TILE_V, width), jnp.float32),
        in_specs=[vmem] * 3,
        out_specs=vmem,
        scratch_shapes=[pltpu.VMEM((taps, width), jnp.float32)],
        compiler_params=params,
        cost_estimate=cost,
    )(other, table, begun)


def body(visibility, kernel_table, cell_index, tile_index, plane_index, offset_index):
    chans, tiles = lax.axis_size("chan"), lax.axis_size("tile")
    packed = pack(chans // 2 * tiles, visibility, cell_index, tile_index[:, 0], plane_index, offset_index, kernel_table)
    chips = [(c, t) for t in range(tiles) for c in range(0, chans, 2)][::-1]
    chips.insert(0, chips.pop(chans // 2))
    groups = [[(c + (side ^ (4 * t >= 3 * tiles))) * tiles + t for c, t in chips] for side in range(2)]
    arrived = lax.all_to_all(
        packed, ("chan", "tile"), split_axis=0, concat_axis=0, axis_index_groups=groups
    )
    swapped = lax.ppermute(arrived, "chan", [(c, c ^ 1) for c in range(chans)])
    return grid(arrived, swapped, kernel_table, chans)


def solution(mesh):
    placed = (
        P(None, ("chan", "tile")),
        P(),
        P(("chan", "tile")),
        P(("chan", "tile"), None),
        P(("chan", "tile")),
        P(("chan", "tile")),
    )
    return jax.shard_map(
        body, mesh=mesh, in_specs=placed, out_specs=P(None, "tile", "chan"), check_vma=False
    )
```

```python
import functools

import jax
import jax.numpy as jnp
from jax import lax
from jax.experimental import pallas as pl
from jax.experimental.pallas import tpu as pltpu
from jax.sharding import PartitionSpec as P

GRID_U = 4096
SUPPORT = 8
OVERSAMPLE = 8
TILE_V = 16
AREA = SUPPORT * SUPPORT
LANES = 128
BLOCK = 2 * LANES
PLAIN = 1
DEEP = 6
SHARE = 16
PIECE = 256


def pack_kernel(*refs):
    far, out_ref, near, sems = refs[:5], refs[6], refs[7:12], refs[12]
    copies = [pltpu.make_async_copy(a, b, sems.at[i]) for i, (a, b) in enumerate(zip(far, near))]
    for copy in copies:
        copy.start()
    for copy in copies:
        copy.wait()
    vis_ref, cell_ref, tile_ref, plane_ref, offset_ref = near
    rows = vis_ref.shape[1]
    address = (tile_ref[...] * (TILE_V * GRID_U) + cell_ref[...]).astype(jnp.float32)
    kind = (plane_ref[...] * (OVERSAMPLE * OVERSAMPLE) + offset_ref[...]).astype(jnp.float32)
    parts = []
    for first in range(0, rows, BLOCK):
        for q in range(2):
            for half in range(2):
                start = first + half * LANES
                parts.append(vis_ref[q : q + 1, start : start + LANES])
        at = first // LANES
        parts.append(address[at : at + 2])
        parts.append(kind[at : at + 2])
    packed = jnp.concatenate(parts, axis=0)

    for d in range(out_ref.shape[0]):
        out_ref[d] = packed


def pack(devices, visibility, cell, tile, plane, offset, table):
    rows = visibility.shape[1]
    flat = [a.reshape(rows // LANES, LANES) for a in (cell, tile, plane, offset)]
    operands = (visibility, *flat)
    return pl.pallas_call(
        pack_kernel,
        out_shape=jax.ShapeDtypeStruct((devices, rows // BLOCK * 8, LANES), jnp.float32),
        in_specs=[pl.BlockSpec(memory_space=pltpu.HBM)] * 6,
        out_specs=pl.BlockSpec(memory_space=pltpu.VMEM),
        scratch_shapes=[pltpu.VMEM(a.shape, a.dtype) for a in operands]
        + [pltpu.SemaphoreType.DMA((len(operands),))],
        compiler_params=pltpu.CompilerParams(vmem_limit_bytes=4 * 1024 * 1024),
    )(*[pltpu.with_memory_space_constraint(a, pltpu.HBM) for a in (*operands, table)])


def along_sublanes(values, index):
    return jnp.take_along_axis(values, index, axis=0, mode="promise_in_bounds")


def iota(shape, axis):
    return lax.broadcasted_iota(jnp.int32, shape, axis)


def dot(a, b, dims):
    return lax.dot_general(a, b, (dims, ((), ())), preferred_element_type=jnp.float32)


class Gridder:
    def __init__(self, width, table_ref):
        self.width = width
        self.first_u = lax.axis_index("chan") * width
        self.first_v = lax.axis_index("tile") * TILE_V
        self.half = iota((8, LANES), 0) & 1
        self.rows_b = iota((256, PIECE), 0).astype(jnp.float32).astype(jnp.bfloat16)
        self.table = [table_ref[k : k + 256, :].T for k in range(0, table_ref.shape[0], 256)]

    def line(self, values):
        return jnp.broadcast_to(values.astype(jnp.float32).astype(jnp.bfloat16), (256, PIECE))

    def sums(self, tiles):
        width, one, zero = self.width, jnp.bfloat16(1), jnp.bfloat16(0)
        spreads, places = [], []
        for tile in tiles:
            vr, vi, address, kind = [
                jnp.concatenate([tile[2 * q : 2 * q + 1], tile[2 * q + 1 : 2 * q + 2]], axis=1) for q in range(4)
            ]
            address = address.astype(jnp.int32)
            kind = kind.astype(jnp.int32)
            u_n = (address & (GRID_U - 1)) - self.first_u
            v_n = (address >> 12) - self.first_v
            high = kind >> 8
            onehot = jnp.where(self.rows_b == self.line(kind & 255), one, zero)
            kern = jnp.zeros((2 * AREA, PIECE), jnp.float32)
            for k, part in enumerate(self.table):
                kern = jnp.where(high == k, dot(part, onehot, ((1,), (0,))), kern)
            real_kern = kern[:AREA]
            imag_kern = kern[AREA:]
            weighted = (vr * real_kern - vi * imag_kern, vr * imag_kern + vi * real_kern)
            sub = iota((SUPPORT, PIECE), 0)
            turn = (sub - v_n) & (SUPPORT - 1)
            inside = [(sub + 8 * y >= v_n) & (sub + 8 * y < v_n + SUPPORT) for y in range(2)]
            spread = []
            for i in range(SUPPORT):
                in_u = (u_n + i >= 0) & (u_n + i < width)
                for c in range(2):
                    turned = along_sublanes(weighted[c][i * 8 : (i + 1) * 8], turn)
                    for y in range(2):
                        spread.append(jnp.where(inside[y] & in_u, turned, 0.0))
            spreads.append(jnp.concatenate(spread, axis=0).astype(jnp.bfloat16))
            column = jnp.where(u_n < 0, u_n + width, u_n)
            near = jnp.where(self.rows_b == self.line(column & 255), one, zero)
            far = self.line(column >> 8)
            place = [jnp.where(far == h, near, zero) for h in range(-(-width // 256))]
            places.append(jnp.concatenate(place, axis=0)[:width])
        return dot(jnp.concatenate(spreads, axis=1), jnp.concatenate(places, axis=1), ((1,), (1,)))

    def marked(self, rows_ref, first_block, span):
        tiles, ranks = [], []
        total = jnp.zeros((8, LANES), jnp.int32)
        for block in range(span):
            tile = rows_ref[pl.ds((first_block + block) * 8, 8), :]
            address = tile.astype(jnp.int32)
            v_rel = (address >> 12) - self.first_v
            u_rel = (address & (GRID_U - 1)) - self.first_u
            touches = (v_rel > -SUPPORT) & (v_rel < TILE_V) & (u_rel > -SUPPORT) & (u_rel < self.width)
            here = along_sublanes(jnp.where(touches, 1, 0), 4 + self.half)
            ranks.append(jnp.where(here > 0, total, -1))
            tiles.append(tile)
            total = total + here
        return tiles, ranks, total

    def later_sections(self, rows_ref, span, add):
        blocks = rows_ref.shape[0] // 8
        if blocks > span:

            @pl.loop(1, blocks // span)
            def _(section):
                tiles, ranks, total = self.marked(rows_ref, section * span, span)

                @pl.loop(0, (jnp.max(total) + 1) // 2)
                def _(pair):
                    add(self.sums([ranked(tiles, ranks, 2 * pair + e) for e in range(2)]))


def ranked(tiles, ranks, wanted):
    got = jnp.zeros((8, LANES), jnp.float32)
    for tile, rank in zip(tiles, ranks):
        got = jnp.where(rank == wanted, tile, got)
    return got


def add_rows(grid, span, rows_ref, begin, add):
    sub, lane = iota((8, LANES), 0), iota((8, LANES), 1)
    half = grid.half
    tiles, ranks, total = grid.marked(rows_ref, 0, span)
    beyond = jnp.maximum(total - PLAIN, 0)
    skip = jnp.zeros_like(beyond)
    every = beyond
    for by in range(SHARE, LANES, SHARE):
        earlier = pltpu.roll(beyond, by, axis=1)
        skip = skip + jnp.where(lane >= by, earlier, 0)
        every = every + earlier
    skip = skip + jnp.where(half > 0, along_sublanes(every, sub ^ 1), 0)
    plain = [ranked(tiles, ranks, r) for r in range(PLAIN)]
    more = [ranked(tiles, ranks, r) for r in range(PLAIN, DEEP)]
    slots = 2 * LANES // SHARE
    moved = []
    for slot in range(slots):
        got = jnp.zeros((8, LANES), jnp.float32)
        for k, tile in enumerate(more):
            got = jnp.where(skip == slot - k, tile, got)
        moved.append(got)
    folded = []
    for even, odd in zip(moved[::2], moved[1::2]):
        folded.append(jnp.where(half == 0, even, odd) + along_sublanes(jnp.where(half == 0, odd, even), sub ^ 1))
    groups = len(folded)
    shared = jnp.zeros((8, LANES), jnp.float32)
    for by in range(groups):
        parts = folded[by]
        for f in range(1, groups):
            parts = jnp.where(lane // SHARE == f, folded[(f + by) % groups], parts)
        shared = shared + (pltpu.roll(parts, by * SHARE, axis=1) if by else parts)
    begin(grid.sums([*plain, shared]))
    done = jnp.clip(PLAIN + slots - skip, PLAIN, DEEP)

    @pl.loop(0, (jnp.max(total - done) + 1) // 2)
    def _(pair):
        add(grid.sums([ranked(tiles, ranks, done + (2 * pair + e)) for e in range(2)]))

    grid.later_sections(rows_ref, span, add)


def first_kernel(span, rows_ref, table_ref, sums_ref):
    def begin(sums):
        sums_ref[...] = sums

    def add(sums):
        sums_ref[...] += sums

    add_rows(Gridder(sums_ref.shape[1], table_ref), span, rows_ref, begin, add)


def second_kernel(span, rows_ref, table_ref, begun_ref, out_ref):
    both = 2 * TILE_V

    def along_u(sums):
        result = sums[:both]
        for i in range(1, SUPPORT):
            result = result + pltpu.roll(sums[i * both : (i + 1) * both], i, axis=1)
        return result.reshape(out_ref.shape)

    def begin(sums):
        out_ref[...] = along_u(begun_ref[...] + sums)

    def add(sums):
        out_ref[...] += along_u(sums)

    add_rows(Gridder(out_ref.shape[2], table_ref), span, rows_ref, begin, add)


def grid(own, other, table, chans):
    own, other = [part.reshape(-1, LANES) for part in (own, other)]
    blocks = own.shape[0] // 8
    span = 16 if blocks % 16 == 0 else blocks
    width = GRID_U // chans
    taps = 2 * TILE_V * SUPPORT
    vmem = pl.BlockSpec(memory_space=pltpu.VMEM)
    params = pltpu.CompilerParams(vmem_limit_bytes=16 * 1024 * 1024)
    cost = pl.CostEstimate(flops=10**9, bytes_accessed=10**6, transcendentals=0)
    begun = pl.pallas_call(
        functools.partial(first_kernel, span),
        out_shape=pltpu.VMEM((taps, width), jnp.float32),
        in_specs=[vmem] * 2,
        out_specs=vmem,
        compiler_params=params,
        cost_estimate=cost,
    )(own, table)
    return pl.pallas_call(
        functools.partial(second_kernel, span),
        out_shape=jax.ShapeDtypeStruct((2, TILE_V, width), jnp.float32),
        in_specs=[vmem] * 3,
        out_specs=vmem,
        compiler_params=params,
        cost_estimate=cost,
    )(other, table, begun)


def body(visibility, kernel_table, cell_index, tile_index, plane_index, offset_index):
    chans, tiles = lax.axis_size("chan"), lax.axis_size("tile")
    packed = pack(chans // 2 * tiles, visibility, cell_index, tile_index[:, 0], plane_index, offset_index, kernel_table)
    chips = [(c, t) for t in range(tiles) for c in range(0, chans, 2)][::-1]
    chips.insert(0, chips.pop(chans // 2))
    groups = [[(c + (side ^ (4 * t >= 3 * tiles))) * tiles + t for c, t in chips] for side in range(2)]
    arrived = lax.all_to_all(
        packed, ("chan", "tile"), split_axis=0, concat_axis=0, axis_index_groups=groups
    )
    swapped = lax.ppermute(arrived, "chan", [(c, c ^ 1) for c in range(chans)])
    return grid(arrived, swapped, kernel_table, chans)


def solution(mesh):
    placed = (
        P(None, ("chan", "tile")),
        P(),
        P(("chan", "tile")),
        P(("chan", "tile"), None),
        P(("chan", "tile")),
        P(("chan", "tile")),
    )
    return jax.shard_map(
        body, mesh=mesh, in_specs=placed, out_specs=P(None, "tile", "chan"), check_vma=False
    )
```
